32 devices in a mesh: state: 8 (over y, x, core), obs: 4 (over z).
Axes of the slice: x: 2, y: 2, z: 4, core: 2. Of those that a mesh axis runs over, the one named last changes fastest.
Arguments:
- predictions: bfloat16 [16384, 1024], P(('state', 'obs')), may hold values from -6 to 6
- obs_index: int32 [16384], P(('state', 'obs')), may hold values from 0 to 16383, as said below
- data_values: float32 [16384], P(('state', 'obs')), may hold values from -6 to 6
- noise_var: float32 [16384], P(('state', 'obs')), may hold values from 16 to 256
- perturbations: bfloat16 [16384, 1024], P(('state', 'obs')), may hold values from -6 to 6
- unknowns: bfloat16 [65536, 1024], P(('state', 'obs')), may hold values from -6 to 6
Outputs:
- updated: bfloat16 [65536, 1024], P(('state', 'obs'))
- innovation_var: float32 [16384], P(('state', 'obs'))
The draws below stay inside these ranges and needn't reach their ends.
Inputs may be any that keep to these rules, and one draw needn't show every extreme that they name: `obs_index`: every observation 0 to 16383 appears exactly once. Observation k belongs to device k // 512 of the joined state+obs axis. Of the 512 entries of one device, at most 32 belong to any one owner, and in every draw some device has exactly 32 entries for some owner.
All inputs are finite; a program needn't handle non-finite values.
Results may differ from the reference program's by a relative error of at most 0.007.
Values may be sent and summed in bfloat16 or wider, within the bound.
No kernel may reach another device: no remote copies, remote signals or barrier semaphores. Data moves between devices by JAX's collectives and lax.ppermute only.
A program may use at most 128 MiB of HBM per device.

```python
import math
import jax
import jax.numpy as jnp
from jax import lax

MEMBERS = 1024
OBS_DEV = 512
UNK_DEV = 2048
SHARDS = 32
OBSERVATIONS = 16384
UNKNOWNS = 65536


def draw_obs_index(key, part):
    shard_count = SHARDS
    row_count = OBS_DEV
    base_count = row_count // shard_count
    top_count = 2 * base_count
    walk_steps = 4 * shard_count * shard_count
    key_first, key_walk, key_slots, key_rows = jax.random.split(key, 4)
    first_keys = jax.random.split(key_first, 4)
    fixed_row = jax.random.randint(first_keys[0], (), 0, shard_count).astype(jnp.int32)
    other_row = ((fixed_row + jax.random.randint(first_keys[1], (), 1, shard_count)) % shard_count).astype(jnp.int32)
    first_col = jax.random.randint(first_keys[2], (), 0, shard_count).astype(jnp.int32)
    second_col = ((first_col + jax.random.randint(first_keys[3], (), 1, shard_count)) % shard_count).astype(jnp.int32)
    counts = jnp.full((shard_count, shard_count), base_count, jnp.int32)
    counts = counts.at[fixed_row, first_col].add(base_count)
    counts = counts.at[other_row, second_col].add(base_count)
    counts = counts.at[fixed_row, second_col].add(-base_count)
    counts = counts.at[other_row, first_col].add(-base_count)
    walk_keys = jax.random.split(key_walk, 5)
    pick_one = jax.random.randint(walk_keys[0], (walk_steps,), 0, shard_count - 1).astype(jnp.int32)
    pick_two = ((pick_one + jax.random.randint(walk_keys[1], (walk_steps,), 1, shard_count - 1)) % (shard_count - 1)).astype(jnp.int32)
    rows_one = ((fixed_row + 1 + pick_one) % shard_count).astype(jnp.int32)
    rows_two = ((fixed_row + 1 + pick_two) % shard_count).astype(jnp.int32)
    cols_one = jax.random.randint(walk_keys[2], (walk_steps,), 0, shard_count).astype(jnp.int32)
    cols_two = ((cols_one + jax.random.randint(walk_keys[3], (walk_steps,), 1, shard_count)) % shard_count).astype(jnp.int32)
    signs = (2 * jax.random.randint(walk_keys[4], (walk_steps,), 0, 2) - 1).astype(jnp.int32)

    def walk(step, matrix):
        row_a = rows_one[step]
        row_b = rows_two[step]
        col_a = cols_one[step]
        col_b = cols_two[step]
        sign = signs[step]
        raise_a = matrix[row_a, col_a] + sign
        raise_b = matrix[row_b, col_b] + sign
        lower_a = matrix[row_a, col_b] - sign
        lower_b = matrix[row_b, col_a] - sign
        valid = (raise_a >= 0) & (raise_a <= top_count) & (raise_b >= 0) & (raise_b <= top_count)
        valid = valid & (lower_a >= 0) & (lower_a <= top_count) & (lower_b >= 0) & (lower_b <= top_count)
        delta = jnp.where(valid, sign, 0).astype(jnp.int32)
        matrix = matrix.at[row_a, col_a].add(delta)
        matrix = matrix.at[row_b, col_b].add(delta)
        matrix = matrix.at[row_a, col_b].add(-delta)
        matrix = matrix.at[row_b, col_a].add(-delta)
        return matrix
    counts = lax.fori_loop(0, walk_steps, walk, counts)
    row_ends = jnp.cumsum(counts, axis=1).astype(jnp.int32)
    row_starts = row_ends - counts
    col_starts = (jnp.cumsum(counts, axis=0) - counts).astype(jnp.int32)
    columns = jnp.arange(row_count, dtype=jnp.int32)
    owners = jnp.sum((row_ends[:, :, None] <= columns[None, None, :]).astype(jnp.int32), axis=1).astype(jnp.int32)
    within = columns[None, :] - jnp.take_along_axis(row_starts, owners, axis=1)
    position = jnp.take_along_axis(col_starts, owners, axis=1) + within
    slot_perm = jax.vmap(lambda subkey: jax.random.permutation(subkey, row_count))(jax.random.split(key_slots, shard_count)).astype(jnp.int32)
    obs_ids = owners * row_count + slot_perm[owners, position]
    senders = jnp.arange(shard_count, dtype=jnp.int32)[:, None]
    row_perm = jax.vmap(lambda subkey: jax.random.permutation(subkey, row_count))(jax.random.split(key_rows, shard_count)).astype(jnp.int32)
    placed = jnp.zeros((shard_count, row_count), jnp.int32).at[senders, row_perm].set(obs_ids)
    return placed.reshape(-1)


def steps_of(stream_key, extent, cuts, least, high):
    def one(dim, parts):
        steps = jax.random.uniform(jax.random.fold_in(jax.random.fold_in(stream_key, 6), dim), (parts,), jnp.float32, least / len(cuts), high / len(cuts))
        return jnp.repeat(jnp.exp(steps), extent[dim] // parts).reshape((-1,) + (1,) * (len(extent) - dim - 1))

    factor_of = one(*cuts[0])
    for cut in cuts[1:]:
        factor_of = factor_of * one(*cut)
    return factor_of


def noise(own_key, extent, width, bound, cuts=(), kind=jnp.bfloat16):
    level = steps_of(own_key, extent, cuts, -0.22, 0.18) if cuts else 1.0
    result = jax.random.normal(own_key, extent, jnp.float32) * width * level
    return jnp.minimum(jnp.maximum(result, -bound), bound).astype(kind)


def setup_inputs(seed: int = 0) -> dict:
    arg_keys = jax.random.split(jax.random.key(seed), 7)
    return {
        "predictions": noise(arg_keys[0], (OBSERVATIONS, MEMBERS), 1.0, 6.0, ((0, 32),)),
        "obs_index": draw_obs_index(jax.random.fold_in(arg_keys[6], 71), 0),
        "data_values": noise(arg_keys[2], (OBSERVATIONS,), 1.0, 6.0, ((0, 32),), jnp.float32),
        "noise_var": jnp.clip(jnp.exp(math.log(256.0) - 2.7725887 * jax.random.uniform(arg_keys[3], (OBSERVATIONS,), jnp.float32) ** steps_of(arg_keys[3], (OBSERVATIONS,), ((0, 32),), -0.2, 0.2)), 16.0, 256.0),
        "perturbations": noise(arg_keys[4], (OBSERVATIONS, MEMBERS), 1.0, 6.0, ((0, 32),)),
        "unknowns": noise(arg_keys[5], (UNKNOWNS, MEMBERS), 1.0, 6.0, ((0, 32),)),
    }


def reference(predictions, obs_index, data_values, noise_var, perturbations, unknowns):
    arranged = jnp.zeros_like(predictions).at[obs_index].set(predictions)
    pred_vals = arranged.astype(jnp.float32)
    row_mean = lax.optimization_barrier(jnp.mean(pred_vals, axis=1, keepdims=True))
    root_weight = jnp.sqrt(1.0 / noise_var)[:, None]
    anomalies = (root_weight * (pred_vals - row_mean)).astype(jnp.bfloat16)
    raw_innov = data_values[:, None] + perturbations.astype(jnp.float32) - pred_vals
    innovation_var = lax.optimization_barrier(jnp.mean(raw_innov * raw_innov, axis=1))
    innovation = (root_weight * raw_innov).astype(jnp.bfloat16)
    gram = jnp.dot(anomalies.T.astype(jnp.float32), anomalies.astype(jnp.float32), preferred_element_type=jnp.float32)
    cross = jnp.dot(anomalies.T.astype(jnp.float32), innovation.astype(jnp.float32), preferred_element_type=jnp.float32)
    system = gram + (MEMBERS - 1) * jnp.eye(MEMBERS, dtype=jnp.float32)
    factor = jnp.linalg.cholesky(system)
    gain_matrix = jax.scipy.linalg.cho_solve((factor, True), cross).astype(jnp.bfloat16)

    def update_block(block):
        block_vals = block.astype(jnp.float32)
        member_mean = lax.optimization_barrier(jnp.mean(block_vals, axis=1, keepdims=True))
        spread = (block_vals - member_mean).astype(jnp.bfloat16)
        moved = jnp.dot(spread.astype(jnp.float32), gain_matrix.astype(jnp.float32), preferred_element_type=jnp.float32)
        return (block_vals + moved).astype(jnp.bfloat16)
    blocks = unknowns.reshape(SHARDS, UNK_DEV, MEMBERS)
    updated = lax.map(update_block, blocks).reshape(UNKNOWNS, MEMBERS)
    return (updated, innovation_var)
```

```python
import functools
import jax
import jax.numpy as jnp
from jax import lax
from jax.experimental import pallas as pl
from jax.experimental.pallas import tpu as pltpu
from jax.sharding import PartitionSpec as P

AXES = ("state", "obs")
TILE = 256
TOLERANCE = 1e-4
MAX_STEPS = 4096
REFRESH = 32


def bits_of(axis):
    return [(axis, b) for b in range(lax.axis_size(axis).bit_length() - 1)]


def my_bit(dim):
    axis, b = dim
    return (lax.axis_index(axis) >> b) & 1


def swap(vals, dim):
    axis, b = dim
    return lax.ppermute(vals, axis, [(i, i ^ (1 << b)) for i in range(lax.axis_size(axis))])


def pick(vals, bit):
    half = vals.shape[0] // 2
    return lax.dynamic_slice_in_dim(vals, bit * half, half, 0)


def sum_scatter(vals, dims):
    for dim in dims:
        bit = my_bit(dim)
        vals = pick(vals, bit) + swap(pick(vals, 1 - bit), dim)
    return vals


def join(vals, dims):
    for dim in reversed(dims):
        other = swap(vals, dim)
        low = my_bit(dim) == 0
        vals = jnp.concatenate([jnp.where(low, vals, other), jnp.where(low, other, vals)])
    return vals


def orders():
    state, obs = bits_of("state"), bits_of("obs")
    return (state + obs, state[:1] + state[1:][::-1] + obs)


def tile_starts(members):
    starts, at = [], 0
    for j in range(members // TILE):
        starts.append(at)
        at += members - j * TILE
    return starts, at


def solve_kernel(tiles_ref, rhs_ref, out_ref, s1_ref, s2_ref, s3_ref, diag_ref):
    count, members = rhs_ref.shape
    shift = float(members - 1)
    starts, _ = tile_starts(members)
    blocks = members // TILE
    row = lax.broadcasted_iota(jnp.int32, (TILE, TILE), 0)
    col = lax.broadcasted_iota(jnp.int32, (TILE, TILE), 1)

    def place(vals, i, j):
        here = (pl.ds(i * TILE, TILE), pl.ds(j * TILE, TILE))
        one = vals.astype(jnp.bfloat16)
        rest = vals - one.astype(jnp.float32)
        two = rest.astype(jnp.bfloat16)
        s1_ref[here] = one
        s2_ref[here] = two
        s3_ref[here] = (rest - two.astype(jnp.float32)).astype(jnp.bfloat16)

    for j in range(blocks):
        for i in range(j, blocks):
            vals = tiles_ref[pl.ds(starts[j] + (i - j) * TILE, TILE), :]
            if i == j:
                vals = vals + jnp.where(row == col, shift, 0.0)
                diag_ref[:, pl.ds(j * TILE, TILE)] = jnp.sum(jnp.where(row == col, vals, 0.0), axis=0, keepdims=True)
                place(vals, j, j)
            else:
                place(vals, i, j)
                place(vals.T, j, i)

    def times(vals):
        one = vals.astype(jnp.bfloat16)
        rest = vals - one.astype(jnp.float32)
        two = rest.astype(jnp.bfloat16)
        three = (rest - two.astype(jnp.float32)).astype(jnp.bfloat16)
        dot = functools.partial(jnp.dot, preferred_element_type=jnp.float32)
        first = dot(jnp.concatenate([one, two, three]), s1_ref[...])
        second = dot(jnp.concatenate([one, two]), s2_ref[...])
        third = dot(one, s3_ref[...])
        small = first[2 * count :] + second[count:] + third
        return first[:count] + (first[count : 2 * count] + second[:count] + small)

    inverse = 1.0 / diag_ref[...]
    rhs = rhs_ref[...]
    bound = (TOLERANCE * shift) ** 2

    def unsolved(x, r):
        gap = jnp.sum(r * r, axis=1, keepdims=True) - bound * jnp.sum(x * x, axis=1, keepdims=True)
        return jnp.max(gap)

    def divide(a, b):
        return jnp.where(b > 0.0, a / jnp.where(b > 0.0, b, 1.0), 0.0)

    x = rhs * inverse
    r = rhs - times(x)
    z = r * inverse

    def more(carry):
        step, gap = carry[0], carry[1]
        return jnp.logical_and(step < MAX_STEPS, gap > 0.0)

    def advance(carry):
        step, _, x, r, p, rz = carry
        q = times(p)
        alpha = divide(rz, jnp.sum(p * q, axis=1, keepdims=True))
        x = x + alpha * p
        r = r - alpha * q
        r = lax.cond(step % REFRESH == REFRESH - 1, lambda x, r: rhs - times(x), lambda x, r: r, x, r)
        z = r * inverse
        rz_next = jnp.sum(r * z, axis=1, keepdims=True)
        p = z + divide(rz_next, rz) * p
        return step + 1, unsolved(x, r), x, r, p, rz_next

    init = (jnp.int32(0), unsolved(x, r), x, r, z, jnp.sum(r * z, axis=1, keepdims=True))
    out_ref[...] = lax.while_loop(more, advance, init)[2].astype(jnp.bfloat16)


def solve(tiles, rhs):
    members = rhs.shape[1]
    square = pltpu.VMEM((members, members), jnp.bfloat16)
    return pl.pallas_call(
        solve_kernel,
        out_shape=jax.ShapeDtypeStruct(rhs.shape, jnp.bfloat16),
        in_specs=[pl.BlockSpec(memory_space=pltpu.VMEM)] * 2,
        out_specs=pl.BlockSpec(memory_space=pltpu.VMEM),
        scratch_shapes=[square, square, square, pltpu.VMEM((1, members), jnp.float32)],
        compiler_params=pltpu.CompilerParams(vmem_limit_bytes=40 * 1024 * 1024),
        cost_estimate=pl.CostEstimate(flops=6 * 6 * 2 * rhs.shape[0] * members * members, bytes_accessed=6 * members * members, transcendentals=0),
        name="member_solve",
    )(tiles, rhs)


def weighted(vals, root_weight):
    member_mean = jnp.mean(vals, axis=1, keepdims=True)
    return (root_weight * (vals - member_mean)).astype(jnp.bfloat16)


def on_device(predictions, obs_index, data_values, noise_var, perturbations, unknowns):
    shards = lax.axis_size(AXES)
    rows, members = predictions.shape
    capacity = 2 * rows // shards
    me = lax.axis_index(AXES)
    first, second = orders()
    f32, bf16 = jnp.float32, jnp.bfloat16
    ids = jnp.arange(rows, dtype=jnp.int32)
    shard_ids = jnp.arange(shards, dtype=jnp.int32)
    earlier = (ids[:, None] < ids[None, :]).astype(bf16)

    owners, slots = obs_index // rows, obs_index % rows
    by_owner = (shard_ids[:, None] == owners[None, :]).astype(bf16)
    ahead = jnp.dot(by_owner, earlier, preferred_element_type=f32)
    rank = jnp.sum(ahead * by_owner.astype(f32), axis=0).astype(jnp.int32)
    place = owners * capacity + rank
    pack = (jnp.arange(shards * capacity, dtype=jnp.int32)[:, None] == place[None, :]).astype(bf16)
    outgoing = jnp.dot(pack, predictions, preferred_element_type=f32).astype(bf16)
    got = lax.all_to_all(outgoing.reshape(shards, capacity, members), AXES, split_axis=0, concat_axis=0, tiled=True)

    own = jnp.stack([obs_index.astype(f32), noise_var])[None]
    table = join(own, (bits_of("obs") + bits_of("state"))[::-1])
    index_table, noise_table = table[:, 0].astype(jnp.int32), table[:, 1]

    noise_rows = jnp.dot(by_owner.T.astype(f32), noise_table, precision=lax.Precision.HIGHEST, preferred_element_type=f32)
    noise_here = jnp.sum(jnp.where(slots[:, None] == ids[None, :], noise_rows, 0.0), axis=1, keepdims=True)
    here = weighted(predictions.astype(f32), jnp.sqrt(1.0 / noise_here))
    tiles = jnp.concatenate(
        [
            jnp.dot(here[:, j:].T, here[:, j : j + TILE], preferred_element_type=f32)
            for j in range(0, members, TILE)
        ]
    )
    half = tiles.shape[0] // 2
    gram = jnp.concatenate(
        [join(sum_scatter(tiles[:half], first), first), join(sum_scatter(tiles[half:], second), second)]
    )

    mine = index_table // rows == me
    mine_ahead = jnp.dot(mine.astype(bf16), earlier, preferred_element_type=f32).astype(jnp.int32)
    chosen = mine[:, None, :] & (mine_ahead[:, None, :] == jnp.arange(capacity, dtype=jnp.int32)[None, :, None])
    slot_of = jnp.sum(jnp.where(chosen, index_table[:, None, :] % rows + 1, 0), axis=2).reshape(1, -1) - 1
    unpack = (ids[:, None] == slot_of).astype(bf16)
    arranged = jnp.dot(unpack, got.reshape(-1, members), preferred_element_type=f32).astype(bf16)

    pred_vals = arranged.astype(f32)
    root_weight = jnp.sqrt(1.0 / noise_var)[:, None]
    anomalies = weighted(pred_vals, root_weight)
    raw_innov = data_values[:, None] + perturbations.astype(f32) - pred_vals
    innovation_var = jnp.mean(raw_innov * raw_innov, axis=1)
    innovation = (root_weight * raw_innov).astype(bf16)

    bit = my_bit(first[0])
    quarter = members // 4

    def cross_part(stream, side):
        cols = lax.dynamic_slice_in_dim(innovation, stream * 2 * quarter + side * quarter, quarter, 1)
        return jnp.dot(cols.T, anomalies, preferred_element_type=f32)

    sent = [swap(cross_part(s, 1 - bit), first[0]) for s in range(2)]
    kept = [cross_part(s, bit) for s in range(2)]
    cross = [
        sum_scatter(k + g, order[1:]) for k, g, order in zip(kept, sent, (first, second), strict=True)
    ]
    each = cross[0].shape[0]
    gain = solve(gram, jnp.concatenate(cross))
    gain_t = jnp.concatenate([join(gain[:each], first), join(gain[each:], second)])

    block_vals = unknowns.astype(f32)
    spread = (block_vals - jnp.mean(block_vals, axis=1, keepdims=True)).astype(bf16)
    moved = lax.dot_general(spread, gain_t, (((1,), (1,)), ((), ())), preferred_element_type=f32)
    return ((block_vals + moved).astype(bf16), innovation_var)


def solution(mesh):
    return jax.shard_map(
        on_device,
        mesh=mesh,
        in_specs=(
            P(AXES, None),
            P(AXES),
            P(AXES),
            P(AXES),
            P(AXES, None),
            P(AXES, None),
        ),
        out_specs=(P(AXES, None), P(AXES)),
        check_vma=False,
    )
```

```python
import functools
import jax
import jax.numpy as jnp
from jax import lax
from jax.experimental import pallas as pl
from jax.experimental.pallas import tpu as pltpu
from jax.sharding import PartitionSpec as P

AXES = ("state", "obs")
TILE = 256
TOLERANCE = 1e-4
MAX_STEPS = 4096
REFRESH = 32
HOLD = 4


def bits_of(axis):
    return [(axis, b) for b in range(lax.axis_size(axis).bit_length() - 1)]


def my_bit(dim):
    axis, b = dim
    return (lax.axis_index(axis) >> b) & 1


def swap(vals, dim):
    axis, b = dim
    return lax.ppermute(vals, axis, [(i, i ^ (1 << b)) for i in range(lax.axis_size(axis))])


def halves(vals, bit):
    half = vals.shape[1] // 2
    return tuple(lax.dynamic_slice_in_dim(vals, b * half, half, 1) for b in (bit, 1 - bit))


def halve(vals, dim):
    keep, send = halves(vals, my_bit(dim))
    return keep + swap(send, dim)


def double(vals, dim):
    other = swap(vals, dim)
    low = my_bit(dim) == 0
    return jnp.concatenate([jnp.where(low, vals, other), jnp.where(low, other, vals)], axis=1)


def stages():
    state, obs = bits_of("state"), bits_of("obs")
    return state[0], (state[1:], state[1:][::-1]), obs


def merged(parts):
    return parts[0] if len(parts) == 1 else jnp.concatenate(parts)


def parted(parts):
    return parts if len(parts) == 2 else (parts[0][:1], parts[0][1:])


def steps_of(exchange):
    head, middle, tail = stages()

    def both(dim):
        return lambda parts: (exchange(merged(parts), dim),)

    def each(dims):
        return lambda parts: tuple(exchange(v, dim) for v, dim in zip(parted(parts), dims, strict=True))

    return [both(head)] + [each(dims) for dims in zip(*middle, strict=True)] + [both(dim) for dim in tail]


def join(vals):
    parts = (vals,)
    for step in reversed(steps_of(double)):
        parts = step(parts)
    return merged(parts)


def after(vals, first):
    return lax.optimization_barrier((vals, first))[0]


def tile_starts(members):
    starts, at = [], 0
    for j in range(members // TILE):
        starts.append(at)
        at += members - j * TILE
    return starts, at


def solve_kernel(tiles_ref, rhs_ref, out_ref, s1_ref, s2_ref, s3_ref, diag_ref):
    count, members = rhs_ref.shape
    shift = float(members - 1)
    starts, _ = tile_starts(members)
    blocks = members // TILE
    row = lax.broadcasted_iota(jnp.int32, (TILE, TILE), 0)
    col = lax.broadcasted_iota(jnp.int32, (TILE, TILE), 1)

    def place(vals, i, j):
        here = (pl.ds(i * TILE, TILE), pl.ds(j * TILE, TILE))
        one = vals.astype(jnp.bfloat16)
        rest = vals - one.astype(jnp.float32)
        two = rest.astype(jnp.bfloat16)
        s1_ref[here] = one
        s2_ref[here] = two
        s3_ref[here] = (rest - two.astype(jnp.float32)).astype(jnp.bfloat16)

    for j in range(blocks):
        for i in range(j, blocks):
            vals = tiles_ref[pl.ds(starts[j] + (i - j) * TILE, TILE), :]
            if i == j:
                vals = vals + jnp.where(row == col, shift, 0.0)
                diag_ref[:, pl.ds(j * TILE, TILE)] = jnp.sum(jnp.where(row == col, vals, 0.0), axis=0, keepdims=True)
                place(vals, j, j)
            else:
                place(vals, i, j)
                place(vals.T, j, i)

    def times(vals):
        one = vals.astype(jnp.bfloat16)
        rest = vals - one.astype(jnp.float32)
        two = rest.astype(jnp.bfloat16)
        three = (rest - two.astype(jnp.float32)).astype(jnp.bfloat16)
        dot = functools.partial(jnp.dot, preferred_element_type=jnp.float32)
        first = dot(jnp.concatenate([one, two, three]), s1_ref[...])
        second = dot(jnp.concatenate([one, two]), s2_ref[...])
        third = dot(one, s3_ref[...])
        small = first[2 * count :] + second[count:] + third
        return first[:count] + (first[count : 2 * count] + second[:count] + small)

    inverse = 1.0 / diag_ref[...]
    rhs = rhs_ref[...]
    bound = (TOLERANCE * shift) ** 2

    def unsolved(x, r):
        gap = jnp.sum(r * r, axis=1, keepdims=True) - bound * jnp.sum(x * x, axis=1, keepdims=True)
        return jnp.max(gap)

    def divide(a, b):
        return jnp.where(b > 0.0, a / jnp.where(b > 0.0, b, 1.0), 0.0)

    x = rhs * inverse
    r = rhs - times(x)
    z = r * inverse

    def more(carry):
        step, gap = carry[0], carry[1]
        return jnp.logical_and(step < MAX_STEPS, gap > 0.0)

    def advance(carry):
        step, _, x, r, p, rz = carry
        q = times(p)
        alpha = divide(rz, jnp.sum(p * q, axis=1, keepdims=True))
        x = x + alpha * p
        r = r - alpha * q
        r = lax.cond(step % REFRESH == REFRESH - 1, lambda x, r: rhs - times(x), lambda x, r: r, x, r)
        z = r * inverse
        rz_next = jnp.sum(r * z, axis=1, keepdims=True)
        p = z + divide(rz_next, rz) * p
        return step + 1, unsolved(x, r), x, r, p, rz_next

    init = (jnp.int32(0), unsolved(x, r), x, r, z, jnp.sum(r * z, axis=1, keepdims=True))
    out_ref[...] = lax.while_loop(more, advance, init)[2].astype(jnp.bfloat16)


def solve(tiles, rhs):
    members = rhs.shape[1]
    square = pltpu.VMEM((members, members), jnp.bfloat16)
    return pl.pallas_call(
        solve_kernel,
        out_shape=jax.ShapeDtypeStruct(rhs.shape, jnp.bfloat16),
        in_specs=[pl.BlockSpec(memory_space=pltpu.VMEM)] * 2,
        out_specs=pl.BlockSpec(memory_space=pltpu.VMEM),
        scratch_shapes=[square, square, square, pltpu.VMEM((1, members), jnp.float32)],
        compiler_params=pltpu.CompilerParams(vmem_limit_bytes=40 * 1024 * 1024),
        cost_estimate=pl.CostEstimate(flops=6 * 6 * 2 * rhs.shape[0] * members * members, bytes_accessed=6 * members * members, transcendentals=0),
        name="member_solve",
    )(tiles, rhs)


def weighted(vals, root_weight):
    member_mean = jnp.mean(vals, axis=1, keepdims=True)
    return (root_weight * (vals - member_mean)).astype(jnp.bfloat16)


def on_device(predictions, obs_index, data_values, noise_var, perturbations, unknowns):
    shards = lax.axis_size(AXES)
    rows, members = predictions.shape
    capacity = 2 * rows // shards
    me = lax.axis_index(AXES)
    f32, bf16 = jnp.float32, jnp.bfloat16
    ids = jnp.arange(rows, dtype=jnp.int32)
    shard_ids = jnp.arange(shards, dtype=jnp.int32)
    earlier = (ids[:, None] < ids[None, :]).astype(bf16)

    owners, slots = obs_index // rows, obs_index % rows
    by_owner = (shard_ids[:, None] == owners[None, :]).astype(bf16)
    ahead = jnp.dot(by_owner, earlier, preferred_element_type=f32)
    rank = jnp.sum(ahead * by_owner.astype(f32), axis=0).astype(jnp.int32)
    place = owners * capacity + rank
    pack = (jnp.arange(shards * capacity, dtype=jnp.int32)[:, None] == place[None, :]).astype(bf16)
    outgoing = jnp.dot(pack, predictions, preferred_element_type=f32).astype(bf16)
    got = lax.all_to_all(outgoing.reshape(shards, capacity, members), AXES, split_axis=0, concat_axis=0, tiled=True)

    own = jnp.stack([obs_index.astype(f32), noise_var])[None]
    table = lax.all_to_all(jnp.broadcast_to(own, (shards, 2, rows)), AXES, split_axis=0, concat_axis=0, tiled=True)[None]
    table = after(table, outgoing)
    index_table, noise_table = table[0, :, 0].astype(jnp.int32), table[0, :, 1]

    noise_rows = jnp.dot(by_owner.T.astype(f32), noise_table, precision=lax.Precision.HIGHEST, preferred_element_type=f32)
    noise_here = jnp.sum(jnp.where(slots[:, None] == ids[None, :], noise_rows, 0.0), axis=1, keepdims=True)
    here = weighted(predictions.astype(f32), jnp.sqrt(1.0 / noise_here))
    tiles = jnp.concatenate(
        [
            jnp.dot(here[:, j:].T, here[:, j : j + TILE], preferred_element_type=f32)
            for j in range(0, members, TILE)
        ]
    )
    ahead_steps = steps_of(halve) + steps_of(double)[::-1]
    gram = (tiles.reshape(2, -1, TILE),)
    for step in ahead_steps[:HOLD]:
        gram = step(gram)

    mine = index_table // rows == me
    mine_ahead = jnp.dot(mine.astype(bf16), earlier, preferred_element_type=f32).astype(jnp.int32)
    chosen = mine[:, None, :] & (mine_ahead[:, None, :] == jnp.arange(capacity, dtype=jnp.int32)[None, :, None])
    slot_of = jnp.sum(jnp.where(chosen, index_table[:, None, :] % rows + 1, 0), axis=2).reshape(1, -1) - 1
    unpack = (ids[:, None] == slot_of).astype(bf16)
    arranged = jnp.dot(unpack, got.reshape(-1, members), preferred_element_type=f32).astype(bf16)

    pred_vals = arranged.astype(f32)
    root_weight = jnp.sqrt(1.0 / noise_var)[:, None]
    anomalies = weighted(pred_vals, root_weight)
    raw_innov = data_values[:, None] + perturbations.astype(f32) - pred_vals
    innovation_var = jnp.mean(raw_innov * raw_innov, axis=1)
    innovation = (root_weight * raw_innov).astype(bf16)

    head = stages()[0]
    bit = my_bit(head)
    quarter = members // 4

    def cross_part(side):
        cols = jnp.concatenate([lax.dynamic_slice_in_dim(innovation, (2 * s + side) * quarter, quarter, 1) for s in range(2)], axis=1)
        return jnp.dot(cols.T, anomalies, preferred_element_type=f32).reshape(2, -1, members)

    later = iter(ahead_steps[HOLD:])
    gram = next(later)(after(gram, innovation))
    gram, send = lax.optimization_barrier((gram, cross_part(1 - bit)))
    cross = (cross_part(bit) + swap(send, head),)
    gram = next(later)(gram)
    for step in steps_of(halve)[1:]:
        gram, cross = lax.optimization_barrier((gram, cross))
        gram, cross = next(later)(gram), step(cross)
    for step in later:
        gram = step(gram)
    tiles, cross = merged(gram).reshape(-1, TILE), merged(cross)
    gain = solve(tiles, cross.reshape(-1, members))
    gain_t = join(gain.reshape(2, -1, members)).reshape(members, members)

    block_vals = unknowns.astype(f32)
    spread = (block_vals - jnp.mean(block_vals, axis=1, keepdims=True)).astype(bf16)
    moved = lax.dot_general(spread, gain_t, (((1,), (1,)), ((), ())), preferred_element_type=f32)
    return ((block_vals + moved).astype(bf16), innovation_var)


def solution(mesh):
    return jax.shard_map(
        on_device,
        mesh=mesh,
        in_specs=(
            P(AXES, None),
            P(AXES),
            P(AXES),
            P(AXES),
            P(AXES, None),
            P(AXES, None),
        ),
        out_specs=(P(AXES, None), P(AXES)),
        check_vma=False,
    )
```

```python
import functools
import jax
import jax.numpy as jnp
from jax import lax
from jax.experimental import pallas as pl
from jax.experimental.pallas import tpu as pltpu
from jax.sharding import PartitionSpec as P

AXES = ("state", "obs")
TILE = 256
TOLERANCE = 5e-4
MAX_STEPS = 4096
REFRESH = 32
FIRST_STEPS = 3
HOLD = 4


def bits_of(axis):
    return [(axis, b) for b in range(lax.axis_size(axis).bit_length() - 1)]


def my_bit(dim):
    axis, b = dim
    return (lax.axis_index(axis) >> b) & 1


def swap(vals, dim):
    axis, b = dim
    return lax.ppermute(vals, axis, [(i, i ^ (1 << b)) for i in range(lax.axis_size(axis))])


def halves(vals, bit):
    half = vals.shape[1] // 2
    return tuple(lax.dynamic_slice_in_dim(vals, b * half, half, 1) for b in (bit, 1 - bit))


def halve(vals, dim):
    keep, send = halves(vals, my_bit(dim))
    return keep + swap(send, dim)


def double(vals, dim):
    other = swap(vals, dim)
    low = my_bit(dim) == 0
    return jnp.concatenate([jnp.where(low, vals, other), jnp.where(low, other, vals)], axis=1)


def stages():
    state, obs = bits_of("state"), bits_of("obs")
    return state[0], (state[1:], state[1:][::-1]), obs


def merged(parts):
    return parts[0] if len(parts) == 1 else jnp.concatenate(parts)


def parted(parts):
    return parts if len(parts) == 2 else (parts[0][:1], parts[0][1:])


def steps_of(exchange):
    head, middle, tail = stages()

    def both(dim):
        return lambda parts: (exchange(merged(parts), dim),)

    def each(dims):
        return lambda parts: tuple(exchange(v, dim) for v, dim in zip(parted(parts), dims, strict=True))

    return [both(head)] + [each(dims) for dims in zip(*middle, strict=True)] + [both(dim) for dim in tail]


def after(vals, first):
    return lax.optimization_barrier((vals, first))[0]


def tile_starts(members):
    starts, at = [], 0
    for j in range(members // TILE):
        starts.append(at)
        at += members - j * TILE
    return starts, at


def solve_kernel(bit_ref, near_ref, far_ref, rhs_ref, out_ref, tiles_ref, s1_ref, s2_ref, s3_ref, diag_ref):
    count, members = rhs_ref.shape
    shift = float(members - 1)
    starts, _ = tile_starts(members)
    blocks = members // TILE
    row = lax.broadcasted_iota(jnp.int32, (TILE, TILE), 0)
    col = lax.broadcasted_iota(jnp.int32, (TILE, TILE), 1)

    def place(vals, i, j):
        here = (pl.ds(i * TILE, TILE), pl.ds(j * TILE, TILE))
        one = vals.astype(jnp.bfloat16)
        rest = vals - one.astype(jnp.float32)
        two = rest.astype(jnp.bfloat16)
        s1_ref[here] = one
        s2_ref[here] = two
        s3_ref[here] = (rest - two.astype(jnp.float32)).astype(jnp.bfloat16)

    streams, half, _ = near_ref.shape
    for s in range(streams):
        for side, ref in ((bit_ref[0], near_ref), (1 - bit_ref[0], far_ref)):
            tiles_ref[pl.ds(pl.multiple_of((2 * s + side) * half, 8), half), :] = ref[s]

    for j in range(blocks):
        for i in range(j, blocks):
            vals = tiles_ref[pl.ds(starts[j] + (i - j) * TILE, TILE), :]
            if i == j:
                on = jnp.where(row == col, vals, 0.0)
                diag_ref[:, pl.ds(j * TILE, TILE)] = jnp.sum(on, axis=0, keepdims=True) + shift
                place(vals - on, j, j)
            else:
                place(vals, i, j)
                place(vals.T, j, i)

    diag = diag_ref[...]
    inverse = 1.0 / diag
    rhs = rhs_ref[...]
    dot = functools.partial(jnp.dot, preferred_element_type=jnp.float32)

    def split(vals):
        one = vals.astype(jnp.bfloat16)
        rest = vals - one.astype(jnp.float32)
        return one, rest.astype(jnp.bfloat16), rest

    def times(vals):
        one, two, rest = split(vals)
        three = (rest - two.astype(jnp.float32)).astype(jnp.bfloat16)
        first = dot(jnp.concatenate([one, two, three]), s1_ref[...])
        second = dot(jnp.concatenate([one, two]), s2_ref[...])
        third = dot(one, s3_ref[...])
        small = first[2 * count :] + second[count:] + third
        return vals * diag + (first[:count] + (first[count : 2 * count] + second[:count] + small))

    def nearly_times(vals):
        one, two, _ = split(vals)
        first = dot(jnp.concatenate([one, two]), s1_ref[...])
        return vals * diag + (first[:count] + first[count:])

    bound = (TOLERANCE * shift) ** 2

    def unsolved(x, r):
        gap = jnp.sum(r * r, axis=1, keepdims=True) - bound * jnp.sum(x * x, axis=1, keepdims=True)
        return jnp.max(gap)

    def divide(a, b):
        return jnp.where(b > 0.0, a / jnp.where(b > 0.0, b, 1.0), 0.0)

    def step_of(product, x, r, p, rz):
        q = product(p)
        alpha = divide(rz, jnp.sum(p * q, axis=1, keepdims=True))
        return x + alpha * p, r - alpha * q

    def turn(r, p, rz):
        z = r * inverse
        rz_next = jnp.sum(r * z, axis=1, keepdims=True)
        return z + divide(rz_next, rz) * p, rz_next

    x, r = jnp.zeros_like(rhs), rhs
    p, rz = turn(r, r, jnp.zeros((count, 1), jnp.float32))
    for i in range(FIRST_STEPS):
        x, r = step_of(nearly_times, x, r, p, rz)
        if i < FIRST_STEPS - 1:
            p, rz = turn(r, p, rz)

    r = rhs - times(x)
    p, rz = turn(r, r, jnp.zeros((count, 1), jnp.float32))

    def more(carry):
        return jnp.logical_and(carry[0] < MAX_STEPS, carry[1] > 0.0)

    def advance(carry):
        step, _, x, r, p, rz = carry
        x, r = step_of(times, x, r, p, rz)
        r = lax.cond(step % REFRESH == REFRESH - 1, lambda x, r: rhs - times(x), lambda x, r: r, x, r)
        p, rz = turn(r, p, rz)
        return step + 1, unsolved(x, r), x, r, p, rz

    x = lax.while_loop(more, advance, (jnp.int32(0), unsolved(x, r), x, r, p, rz))[2]
    out_ref[...] = x.astype(jnp.bfloat16)


def solve(bit, near, far, rhs):
    members = rhs.shape[1]
    square = pltpu.VMEM((members, members), jnp.bfloat16)
    vmem = pl.BlockSpec(memory_space=pltpu.VMEM)
    return pl.pallas_call(
        solve_kernel,
        out_shape=jax.ShapeDtypeStruct(rhs.shape, jnp.bfloat16),
        in_specs=[pl.BlockSpec(memory_space=pltpu.SMEM), vmem, vmem, vmem],
        out_specs=vmem,
        scratch_shapes=[
            pltpu.VMEM((tile_starts(members)[1], TILE), jnp.float32),
            square,
            square,
            square,
            pltpu.VMEM((1, members), jnp.float32),
        ],
        compiler_params=pltpu.CompilerParams(vmem_limit_bytes=40 * 1024 * 1024),
        cost_estimate=pl.CostEstimate(flops=24 * 2 * rhs.shape[0] * members * members, bytes_accessed=6 * members * members, transcendentals=0),
        name="member_solve",
    )(bit, near, far, rhs)


def weighted(vals, root_weight):
    member_mean = jnp.mean(vals, axis=1, keepdims=True)
    return (root_weight * (vals - member_mean)).astype(jnp.bfloat16)


def on_device(predictions, obs_index, data_values, noise_var, perturbations, unknowns):
    shards = lax.axis_size(AXES)
    rows, members = predictions.shape
    capacity = 2 * rows // shards
    me = lax.axis_index(AXES)
    f32, bf16 = jnp.float32, jnp.bfloat16
    ids = jnp.arange(rows, dtype=jnp.int32)
    shard_ids = jnp.arange(shards, dtype=jnp.int32)
    earlier = (ids[:, None] < ids[None, :]).astype(bf16)

    owners, slots = obs_index // rows, obs_index % rows
    by_owner = (shard_ids[:, None] == owners[None, :]).astype(bf16)
    ahead = jnp.dot(by_owner, earlier, preferred_element_type=f32)
    rank = jnp.sum(ahead * by_owner.astype(f32), axis=0).astype(jnp.int32)
    place = owners * capacity + rank
    pack = (jnp.arange(shards * capacity, dtype=jnp.int32)[:, None] == place[None, :]).astype(bf16)
    outgoing = jnp.dot(pack, predictions, preferred_element_type=f32).astype(bf16)
    got = lax.all_to_all(outgoing.reshape(shards, capacity, members), AXES, split_axis=0, concat_axis=0, tiled=True)

    own = jnp.stack([obs_index.astype(f32), noise_var])[None]
    table = lax.all_to_all(jnp.broadcast_to(own, (shards, 2, rows)), AXES, split_axis=0, concat_axis=0, tiled=True)[None]
    table = after(table, outgoing)
    index_table, noise_table = table[0, :, 0].astype(jnp.int32), table[0, :, 1]

    noise_rows = jnp.dot(by_owner.T.astype(f32), noise_table, precision=lax.Precision.HIGHEST, preferred_element_type=f32)
    noise_here = jnp.sum(jnp.where(slots[:, None] == ids[None, :], noise_rows, 0.0), axis=1, keepdims=True)
    here = weighted(predictions.astype(f32), jnp.sqrt(1.0 / noise_here))
    tiles = jnp.concatenate(
        [
            jnp.dot(here[:, j:].T, here[:, j : j + TILE], preferred_element_type=f32)
            for j in range(0, members, TILE)
        ]
    )
    ahead_steps = steps_of(halve) + steps_of(double)[:0:-1]
    gram = (tiles.reshape(2, -1, TILE),)
    for step in ahead_steps[:HOLD]:
        gram = step(gram)

    mine = index_table // rows == me
    mine_ahead = jnp.dot(mine.astype(bf16), earlier, preferred_element_type=f32).astype(jnp.int32)
    chosen = mine[:, None, :] & (mine_ahead[:, None, :] == jnp.arange(capacity, dtype=jnp.int32)[None, :, None])
    slot_of = jnp.sum(jnp.where(chosen, index_table[:, None, :] % rows + 1, 0), axis=2).reshape(1, -1) - 1
    unpack = (ids[:, None] == slot_of).astype(bf16)
    arranged = jnp.dot(unpack, got.reshape(-1, members), preferred_element_type=f32).astype(bf16)

    pred_vals = arranged.astype(f32)
    root_weight = jnp.sqrt(1.0 / noise_var)[:, None]
    anomalies = weighted(pred_vals, root_weight)
    raw_innov = data_values[:, None] + perturbations.astype(f32) - pred_vals
    innovation_var = jnp.mean(raw_innov * raw_innov, axis=1)
    innovation = (root_weight * raw_innov).astype(bf16)

    head = stages()[0]
    bit = my_bit(head)
    wide = members // 2

    def cross_part(side):
        cols = lax.dynamic_slice_in_dim(innovation, side * wide, wide, 1)
        return jnp.dot(cols.T, anomalies, preferred_element_type=f32).reshape(2, -1, members)

    block_vals = unknowns.astype(f32)
    spread = (block_vals - jnp.mean(block_vals, axis=1, keepdims=True)).astype(bf16)

    later = iter(ahead_steps[HOLD:])
    gram, send, spread = lax.optimization_barrier((gram, cross_part(1 - bit), spread))
    cross = (cross_part(bit) + swap(send, head),)
    gram = next(later)(gram)
    for step in steps_of(halve)[1:]:
        gram, cross = lax.optimization_barrier((gram, cross))
        gram, cross = next(later, lambda parts: parts)(gram), step(cross)
    for step in later:
        gram = step(gram)
    near, cross = lax.optimization_barrier((merged(gram), merged(cross)))
    side = jnp.reshape(bit, (1,)).astype(jnp.int32)
    gain = solve(side, near, swap(near, head), cross.reshape(-1, members)).reshape(2, -1, members)

    gain = (gain,)
    for step in steps_of(double)[:0:-1]:
        gain = step(gain)
    gain = merged(gain).reshape(wide, members)
    other = swap(gain, head)

    def side_of(gain, at):
        moved = lax.dot_general(spread, gain, (((1,), (1,)), ((), ())), preferred_element_type=f32)
        return (lax.dynamic_slice_in_dim(unknowns, at, wide, 1).astype(f32) + moved).astype(bf16)

    updated = lax.dynamic_update_slice_in_dim(jnp.zeros_like(unknowns), side_of(gain, bit * wide), bit * wide, 1)
    updated = lax.dynamic_update_slice_in_dim(updated, side_of(other, (1 - bit) * wide), (1 - bit) * wide, 1)
    return (updated, innovation_var)


def solution(mesh):
    return jax.shard_map(
        on_device,
        mesh=mesh,
        in_specs=(
            P(AXES, None),
            P(AXES),
            P(AXES),
            P(AXES),
            P(AXES, None),
            P(AXES, None),
        ),
        out_specs=(P(AXES, None), P(AXES)),
        check_vma=False,
    )
```

```python
import functools
import jax
import jax.numpy as jnp
from jax import lax
from jax.experimental import pallas as pl
from jax.experimental.pallas import tpu as pltpu
from jax.sharding import PartitionSpec as P

AXES = ("state", "obs")
TILE = 256
TOLERANCE = 5e-4
MAX_STEPS = 4096
REFRESH = 32
FIRST_STEPS = 3
HINT = 20000000000
HOLD = 4


def bits_of(axis):
    return [(axis, b) for b in range(lax.axis_size(axis).bit_length() - 1)]


def my_bit(dim):
    axis, b = dim
    return (lax.axis_index(axis) >> b) & 1


def swap(vals, dim):
    axis, b = dim
    return lax.ppermute(vals, axis, [(i, i ^ (1 << b)) for i in range(lax.axis_size(axis))])


def halves(vals, bit):
    half = vals.shape[1] // 2
    return tuple(lax.dynamic_slice_in_dim(vals, b * half, half, 1) for b in (bit, 1 - bit))


def halve(vals, dim):
    keep, send = halves(vals, my_bit(dim))
    return keep + swap(send, dim)


def double(vals, dim):
    other = swap(vals, dim)
    low = my_bit(dim) == 0
    return jnp.concatenate([jnp.where(low, vals, other), jnp.where(low, other, vals)], axis=1)


def gather(vals, axis):
    count, mine = lax.axis_size(axis), lax.axis_index(axis)
    pairs = lambda flip: [(i, i ^ flip) for i in range(count)]
    got = [vals] + [lax.ppermute(vals, axis, pairs(flip)) for flip in range(1, count)]
    bits = count.bit_length() - 1
    in_order = [sum((i >> b & 1) << (bits - 1 - b) for b in range(bits)) for i in range(count)]
    return jnp.concatenate([lax.select_n(mine ^ i, *got) for i in in_order], axis=1)


def stages():
    state, obs = bits_of("state"), bits_of("obs")
    return state[0], (state[1:], state[1:][::-1]), obs


def merged(parts):
    return parts[0] if len(parts) == 1 else jnp.concatenate(parts)


def parted(parts):
    return parts if len(parts) == 2 else (parts[0][:1], parts[0][1:])


def steps_of(exchange):
    head, middle, tail = stages()

    def both(dim):
        return lambda parts: (exchange(merged(parts), dim),)

    def each(dims):
        return lambda parts: tuple(exchange(v, dim) for v, dim in zip(parted(parts), dims, strict=True))

    return [both(head)] + [each(dims) for dims in zip(*middle, strict=True)] + [both(dim) for dim in tail]


def after(vals, first):
    return lax.optimization_barrier((vals, first))[0]


def tile_starts(members):
    starts, at = [], 0
    for j in range(members // TILE):
        starts.append(at)
        at += members - j * TILE
    return starts, at


def solve_kernel(bit_ref, near_ref, far_ref, rhs_ref, out_ref, tiles_ref, s1_ref, s2_ref, s3_ref, diag_ref):
    count, members = rhs_ref.shape
    shift = float(members - 1)
    starts, _ = tile_starts(members)
    blocks = members // TILE
    row = lax.broadcasted_iota(jnp.int32, (TILE, TILE), 0)
    col = lax.broadcasted_iota(jnp.int32, (TILE, TILE), 1)

    def place(vals, i, j):
        here = (pl.ds(i * TILE, TILE), pl.ds(j * TILE, TILE))
        one = vals.astype(jnp.bfloat16)
        rest = vals - one.astype(jnp.float32)
        two = rest.astype(jnp.bfloat16)
        s1_ref[here] = one
        s2_ref[here] = two
        s3_ref[here] = (rest - two.astype(jnp.float32)).astype(jnp.bfloat16)

    streams, half, _ = near_ref.shape
    for s in range(streams):
        for side, ref in ((bit_ref[0], near_ref), (1 - bit_ref[0], far_ref)):
            tiles_ref[pl.ds(pl.multiple_of((2 * s + side) * half, 8), half), :] = ref[s]

    for j in range(blocks):
        for i in range(j, blocks):
            vals = tiles_ref[pl.ds(starts[j] + (i - j) * TILE, TILE), :]
            if i == j:
                on = jnp.where(row == col, vals, 0.0)
                diag_ref[:, pl.ds(j * TILE, TILE)] = jnp.sum(on, axis=0, keepdims=True) + shift
                place(vals - on, j, j)
            else:
                place(vals, i, j)
                place(vals.T, j, i)

    diag = diag_ref[...]
    inverse = 1.0 / diag
    rhs = rhs_ref[...]
    dot = functools.partial(jnp.dot, preferred_element_type=jnp.float32)

    def split(vals):
        one = vals.astype(jnp.bfloat16)
        rest = vals - one.astype(jnp.float32)
        return one, rest.astype(jnp.bfloat16), rest

    def times(vals):
        one, two, rest = split(vals)
        three = (rest - two.astype(jnp.float32)).astype(jnp.bfloat16)
        first = dot(jnp.concatenate([one, two, three]), s1_ref[...])
        second = dot(jnp.concatenate([one, two]), s2_ref[...])
        third = dot(one, s3_ref[...])
        small = first[2 * count :] + second[count:] + third
        return vals * diag + (first[:count] + (first[count : 2 * count] + second[:count] + small))

    def nearly_times(vals):
        one, two, _ = split(vals)
        first = dot(jnp.concatenate([one, two]), s1_ref[...])
        return vals * diag + (first[:count] + first[count:])

    bound = (TOLERANCE * shift) ** 2

    def unsolved(x, r):
        gap = jnp.sum(r * r, axis=1, keepdims=True) - bound * jnp.sum(x * x, axis=1, keepdims=True)
        return jnp.max(gap)

    def divide(a, b):
        return jnp.where(b > 0.0, a / jnp.where(b > 0.0, b, 1.0), 0.0)

    def step_of(product, x, r, p, rz):
        q = product(p)
        alpha = divide(rz, jnp.sum(p * q, axis=1, keepdims=True))
        return x + alpha * p, r - alpha * q

    def turn(r, p, rz):
        z = r * inverse
        rz_next = jnp.sum(r * z, axis=1, keepdims=True)
        return z + divide(rz_next, rz) * p, rz_next

    x, r = jnp.zeros_like(rhs), rhs
    p, rz = turn(r, r, jnp.zeros((count, 1), jnp.float32))
    for i in range(FIRST_STEPS):
        x, r = step_of(nearly_times, x, r, p, rz)
        if i < FIRST_STEPS - 1:
            p, rz = turn(r, p, rz)

    r = rhs - times(x)
    p, rz = turn(r, r, jnp.zeros((count, 1), jnp.float32))

    def more(carry):
        return jnp.logical_and(carry[0] < MAX_STEPS, carry[1] > 0.0)

    def advance(carry):
        step, _, x, r, p, rz = carry
        x, r = step_of(times, x, r, p, rz)
        r = lax.cond(step % REFRESH == REFRESH - 1, lambda x, r: rhs - times(x), lambda x, r: r, x, r)
        p, rz = turn(r, p, rz)
        return step + 1, unsolved(x, r), x, r, p, rz

    x = lax.while_loop(more, advance, (jnp.int32(0), unsolved(x, r), x, r, p, rz))[2]
    out_ref[...] = x.astype(jnp.bfloat16)


def solve(bit, near, far, rhs):
    members = rhs.shape[1]
    square = pltpu.VMEM((members, members), jnp.bfloat16)
    vmem = pl.BlockSpec(memory_space=pltpu.VMEM)
    return pl.pallas_call(
        solve_kernel,
        out_shape=jax.ShapeDtypeStruct(rhs.shape, jnp.bfloat16),
        in_specs=[pl.BlockSpec(memory_space=pltpu.SMEM), vmem, vmem, vmem],
        out_specs=vmem,
        scratch_shapes=[
            pltpu.VMEM((tile_starts(members)[1], TILE), jnp.float32),
            square,
            square,
            square,
            pltpu.VMEM((1, members), jnp.float32),
        ],
        compiler_params=pltpu.CompilerParams(vmem_limit_bytes=20 * 1024 * 1024),
        cost_estimate=pl.CostEstimate(flops=24 * 2 * rhs.shape[0] * members * members, bytes_accessed=6 * members * members, transcendentals=0),
        name="member_solve",
    )(bit, near, far, rhs)


def places_kernel(slot_ref, out_ref):
    ids = lax.broadcasted_iota(jnp.int32, out_ref.shape, 0)
    out_ref[...] = jnp.where(ids == slot_ref[...], 1.0, 0.0).astype(jnp.bfloat16)


def places(slots, rows):
    vmem = pl.BlockSpec(memory_space=pltpu.VMEM)
    return pl.pallas_call(
        places_kernel,
        out_shape=jax.ShapeDtypeStruct((rows, slots.shape[1]), jnp.bfloat16),
        in_specs=[vmem],
        out_specs=vmem,
        cost_estimate=pl.CostEstimate(flops=HINT, bytes_accessed=2 * rows * slots.shape[1], transcendentals=0),
        name="places",
    )(slots)


def weighted(vals, root_weight):
    member_mean = jnp.mean(vals, axis=1, keepdims=True)
    return (root_weight * (vals - member_mean)).astype(jnp.bfloat16)


def on_device(predictions, obs_index, data_values, noise_var, perturbations, unknowns):
    shards = lax.axis_size(AXES)
    rows, members = predictions.shape
    capacity = 2 * rows // shards
    me = lax.axis_index(AXES)
    f32, bf16 = jnp.float32, jnp.bfloat16
    ids = jnp.arange(rows, dtype=jnp.int32)
    shard_ids = jnp.arange(shards, dtype=jnp.int32)
    earlier = (ids[:, None] < ids[None, :]).astype(bf16)

    owners, slots = obs_index // rows, obs_index % rows
    by_owner = (shard_ids[:, None] == owners[None, :]).astype(bf16)
    ahead = jnp.dot(by_owner, earlier, preferred_element_type=f32)
    rank = jnp.sum(ahead * by_owner.astype(f32), axis=0).astype(jnp.int32)
    place = owners * capacity + rank
    pack = (jnp.arange(shards * capacity, dtype=jnp.int32)[:, None] == place[None, :]).astype(bf16)
    outgoing = jnp.dot(pack, predictions, preferred_element_type=f32).astype(bf16)
    got = lax.all_to_all(outgoing.reshape(shards, capacity, members), AXES, split_axis=0, concat_axis=0, tiled=True)

    own = jnp.stack([obs_index.astype(f32), noise_var])[None]
    table = lax.all_to_all(jnp.broadcast_to(own, (shards, 2, rows)), AXES, split_axis=0, concat_axis=0, tiled=True)[None]
    table = after(table, outgoing)
    index_table, noise_table = table[0, :, 0].astype(jnp.int32), table[0, :, 1]

    noise_rows = jnp.dot(by_owner.T.astype(f32), noise_table, precision=lax.Precision.HIGHEST, preferred_element_type=f32)
    noise_here = jnp.sum(jnp.where(slots[:, None] == ids[None, :], noise_rows, 0.0), axis=1, keepdims=True)
    here = weighted(predictions.astype(f32), jnp.sqrt(1.0 / noise_here))
    tiles = jnp.concatenate(
        [
            jnp.dot(here[:, j:].T, here[:, j : j + TILE], preferred_element_type=f32)
            for j in range(0, members, TILE)
        ]
    )
    mine = index_table // rows == me
    mine_ahead = jnp.dot(mine.astype(bf16), earlier, preferred_element_type=f32).astype(jnp.int32)
    chosen = mine[:, None, :] & (mine_ahead[:, None, :] == jnp.arange(capacity, dtype=jnp.int32)[None, :, None])
    slot_of = jnp.sum(jnp.where(chosen, index_table[:, None, :] % rows + 1, 0), axis=2).reshape(1, -1) - 1
    unpack = places(slot_of, rows)
    last = stages()[2][-1]
    ahead_steps = steps_of(halve)[:-1] + [lambda parts: (merged(parts) + swap(merged(parts), last),)] + steps_of(double)[-2:0:-1]
    gram = (tiles.reshape(2, -1, TILE),)
    for i, step in enumerate(ahead_steps[:HOLD]):
        gram = step(gram)
        if i == 0:
            gram = after(gram, unpack)

    arranged = jnp.dot(unpack, got.reshape(-1, members), preferred_element_type=f32).astype(bf16)

    pred_vals = arranged.astype(f32)
    root_weight = jnp.sqrt(1.0 / noise_var)[:, None]
    anomalies = weighted(pred_vals, root_weight)
    raw_innov = data_values[:, None] + perturbations.astype(f32) - pred_vals
    innovation_var = jnp.mean(raw_innov * raw_innov, axis=1)
    innovation = (root_weight * raw_innov).astype(bf16)

    head = stages()[0]
    bit = my_bit(head)
    wide = members // 2

    def cross_part(side):
        cols = lax.dynamic_slice_in_dim(innovation, side * wide, wide, 1)
        return jnp.dot(cols.T, anomalies, preferred_element_type=f32).reshape(2, -1, members)


    later = iter(ahead_steps[HOLD:])
    gram, send = lax.optimization_barrier((gram, cross_part(1 - bit)))
    cross = (cross_part(bit) + swap(send, head),)
    gram = next(later)(gram)
    for i, step in enumerate(steps_of(halve)[1:]):
        cross = step(cross)
        if i == 0:
            gram = after(gram, cross[0])
        gram = next(later, lambda parts: parts)(gram)
    for step in later:
        gram = step(gram)
    near, cross = lax.optimization_barrier((merged(gram), merged(cross)))
    side = jnp.reshape(bit, (1,)).astype(jnp.int32)
    gain = solve(side, near, swap(near, head), cross.reshape(-1, members)).reshape(2, -1, members)

    gain = (gather(gain, "obs"),)
    block = after(unknowns, gain)
    block_vals = block.astype(f32)
    spread = (block_vals - jnp.mean(block_vals, axis=1, keepdims=True)).astype(bf16)
    for step in steps_of(double)[len(stages()[1][0]) : 0 : -1]:
        gain = step(gain)
    gain = merged(gain).reshape(wide, members)
    other = swap(gain, head)

    def side_of(gain, at):
        moved = lax.dot_general(spread, gain, (((1,), (1,)), ((), ())), preferred_element_type=f32)
        return (lax.dynamic_slice_in_dim(block, at, wide, 1).astype(f32) + moved).astype(bf16)

    updated = lax.dynamic_update_slice_in_dim(jnp.zeros_like(unknowns), side_of(gain, bit * wide), bit * wide, 1)
    updated = lax.dynamic_update_slice_in_dim(updated, side_of(other, (1 - bit) * wide), (1 - bit) * wide, 1)
    return (updated, innovation_var)


def solution(mesh):
    return jax.shard_map(
        on_device,
        mesh=mesh,
        in_specs=(
            P(AXES, None),
            P(AXES),
            P(AXES),
            P(AXES),
            P(AXES, None),
            P(AXES, None),
        ),
        out_specs=(P(AXES, None), P(AXES)),
        check_vma=False,
    )
```

```python
import functools
import jax
import jax.numpy as jnp
from jax import lax
from jax.experimental import pallas as pl
from jax.experimental.pallas import tpu as pltpu
from jax.sharding import PartitionSpec as P

AXES = ("state", "obs")
TILE = 256
TOLERANCE = 5e-4
STEPS = 512
ROUNDS = 32
FIRST_STEPS = 4
HINT = 20000000000
HOLD = 4


def bits_of(axis):
    return [(axis, b) for b in range(lax.axis_size(axis).bit_length() - 1)]


def my_bit(dim):
    axis, b = dim
    return (lax.axis_index(axis) >> b) & 1


def swap(vals, dim):
    axis, b = dim
    return lax.ppermute(vals, axis, [(i, i ^ (1 << b)) for i in range(lax.axis_size(axis))])


def halves(vals, bit):
    half = vals.shape[1] // 2
    return tuple(lax.dynamic_slice_in_dim(vals, b * half, half, 1) for b in (bit, 1 - bit))


def halve(vals, dim):
    keep, send = halves(vals, my_bit(dim))
    return keep + swap(send, dim)


def double(vals, dim):
    other = swap(vals, dim)
    low = my_bit(dim) == 0
    return jnp.concatenate([jnp.where(low, vals, other), jnp.where(low, other, vals)], axis=1)


def gather(vals, axis):
    count, mine = lax.axis_size(axis), lax.axis_index(axis)
    pairs = lambda flip: [(i, i ^ flip) for i in range(count)]
    got = [vals] + [lax.ppermute(vals, axis, pairs(flip)) for flip in range(1, count)]
    bits = count.bit_length() - 1
    in_order = [sum((i >> b & 1) << (bits - 1 - b) for b in range(bits)) for i in range(count)]
    return jnp.concatenate([lax.select_n(mine ^ i, *got) for i in in_order], axis=1)


def stages():
    state, obs = bits_of("state"), bits_of("obs")
    return state[0], (state[1:], state[1:][::-1]), obs


def merged(parts):
    return parts[0] if len(parts) == 1 else jnp.concatenate(parts)


def parted(parts):
    return parts if len(parts) == 2 else (parts[0][:1], parts[0][1:])


def steps_of(exchange):
    head, middle, tail = stages()

    def both(dim):
        return lambda parts: (exchange(merged(parts), dim),)

    def each(dims):
        return lambda parts: tuple(exchange(v, dim) for v, dim in zip(parted(parts), dims, strict=True))

    return [both(head)] + [each(dims) for dims in zip(*middle, strict=True)] + [both(dim) for dim in tail]


def after(vals, first):
    return lax.optimization_barrier((vals, first))[0]


def tile_starts(members):
    starts, at = [], 0
    for j in range(members // TILE):
        starts.append(at)
        at += members - j * TILE
    return starts, at


def solve_kernel(bit_ref, near_ref, far_ref, rhs_ref, out_ref, tiles_ref, s1_ref, s2_ref, s3_ref, diag_ref):
    count, members = rhs_ref.shape
    shift = float(members - 1)
    starts, _ = tile_starts(members)
    blocks = members // TILE
    row = lax.broadcasted_iota(jnp.int32, (TILE, TILE), 0)
    col = lax.broadcasted_iota(jnp.int32, (TILE, TILE), 1)

    def place(vals, i, j):
        here = (pl.ds(i * TILE, TILE), pl.ds(j * TILE, TILE))
        one = vals.astype(jnp.bfloat16)
        rest = vals - one.astype(jnp.float32)
        two = rest.astype(jnp.bfloat16)
        s1_ref[here] = one
        s2_ref[here] = two
        s3_ref[here] = (rest - two.astype(jnp.float32)).astype(jnp.bfloat16)

    streams, half, _ = near_ref.shape
    for s in range(streams):
        for side, ref in ((bit_ref[0], near_ref), (1 - bit_ref[0], far_ref)):
            tiles_ref[pl.ds(pl.multiple_of((2 * s + side) * half, 8), half), :] = ref[s]

    for j in range(blocks):
        for i in range(j, blocks):
            vals = tiles_ref[pl.ds(starts[j] + (i - j) * TILE, TILE), :]
            if i == j:
                on = jnp.where(row == col, vals, 0.0)
                diag_ref[:, pl.ds(j * TILE, TILE)] = jnp.sum(on, axis=0, keepdims=True) + shift
                place(vals - on, j, j)
            else:
                place(vals, i, j)
                place(vals.T, j, i)

    diag = diag_ref[...]
    inverse = 1.0 / diag
    rhs = rhs_ref[...]
    dot = functools.partial(jnp.dot, preferred_element_type=jnp.float32)

    def split(vals):
        one = vals.astype(jnp.bfloat16)
        rest = vals - one.astype(jnp.float32)
        return one, rest.astype(jnp.bfloat16), rest

    def times(vals):
        one, two, rest = split(vals)
        three = (rest - two.astype(jnp.float32)).astype(jnp.bfloat16)
        first = dot(jnp.concatenate([one, two, three]), s1_ref[...])
        second = dot(jnp.concatenate([one, two]), s2_ref[...])
        third = dot(one, s3_ref[...])
        small = first[2 * count :] + second[count:] + third
        return vals * diag + (first[:count] + (first[count : 2 * count] + second[:count] + small))

    def nearly_times(vals):
        one, two, _ = split(vals)
        first = dot(jnp.concatenate([one, two]), s1_ref[...])
        return vals * diag + (first[:count] + first[count:])

    bound = (TOLERANCE * shift) ** 2

    def unsolved(x, r):
        gap = jnp.sum(r * r, axis=1, keepdims=True) - bound * jnp.sum(x * x, axis=1, keepdims=True)
        return jnp.max(gap)

    def divide(a, b):
        return jnp.where(b > 0.0, a / jnp.where(b > 0.0, b, 1.0), 0.0)

    def step_of(product, x, r, p, rz):
        q = product(p)
        alpha = divide(rz, jnp.sum(p * q, axis=1, keepdims=True))
        return x + alpha * p, r - alpha * q

    def turn(r, p, rz):
        z = r * inverse
        rz_next = jnp.sum(r * z, axis=1, keepdims=True)
        return z + divide(rz_next, rz) * p, rz_next

    x, r = jnp.zeros_like(rhs), rhs
    p, rz = turn(r, r, jnp.zeros((count, 1), jnp.float32))
    for i in range(FIRST_STEPS):
        x, r = step_of(nearly_times, x, r, p, rz)
        if i < FIRST_STEPS - 1:
            p, rz = turn(r, p, rz)

    def norm(r):
        return jnp.sum(r * r, axis=1, keepdims=True)

    def keep_better(x, r, new_x):
        new_r = rhs - times(new_x)
        better = norm(new_r) < norm(r)
        progress = jnp.max(jnp.where(norm(new_r) < 0.5 * norm(r), 1, 0))
        return jnp.where(better, new_x, x), jnp.where(better, new_r, r), progress

    r = rhs - times(x)

    def more(carry):
        return jnp.logical_and(carry[0] < STEPS, carry[1] > 0.0)

    def advance(carry):
        step, _, x, r, p, rz = carry
        x, r = step_of(times, x, r, p, rz)
        p, rz = turn(r, p, rz)
        return step + 1, unsolved(x, r), x, r, p, rz

    def more_rounds(carry):
        count, gap, progress = carry[:3]
        return jnp.logical_and(jnp.logical_and(count < ROUNDS, gap > 0.0), progress > 0)

    def another(carry):
        count, gap, _, x, r = carry
        p, rz = turn(r, r, jnp.zeros((rhs.shape[0], 1), jnp.float32))
        new_x = lax.while_loop(more, advance, (jnp.int32(0), gap, x, r, p, rz))[2]
        x, r, progress = keep_better(x, r, new_x)
        return count + 1, unsolved(x, r), progress, x, r

    x = lax.while_loop(more_rounds, another, (jnp.int32(0), unsolved(x, r), jnp.int32(1), x, r))[3]
    out_ref[...] = x.astype(jnp.bfloat16)


def solve(bit, near, far, rhs):
    members = rhs.shape[1]
    square = pltpu.VMEM((members, members), jnp.bfloat16)
    vmem = pl.BlockSpec(memory_space=pltpu.VMEM)
    return pl.pallas_call(
        solve_kernel,
        out_shape=jax.ShapeDtypeStruct(rhs.shape, jnp.bfloat16),
        in_specs=[pl.BlockSpec(memory_space=pltpu.SMEM), vmem, vmem, vmem],
        out_specs=vmem,
        scratch_shapes=[
            pltpu.VMEM((tile_starts(members)[1], TILE), jnp.float32),
            square,
            square,
            square,
            pltpu.VMEM((1, members), jnp.float32),
        ],
        compiler_params=pltpu.CompilerParams(vmem_limit_bytes=20 * 1024 * 1024),
        cost_estimate=pl.CostEstimate(flops=24 * 2 * rhs.shape[0] * members * members, bytes_accessed=6 * members * members, transcendentals=0),
        name="member_solve",
    )(bit, near, far, rhs)


def places_kernel(slot_ref, out_ref):
    ids = lax.broadcasted_iota(jnp.int32, out_ref.shape, 0)
    out_ref[...] = jnp.where(ids == slot_ref[...], 1.0, 0.0).astype(jnp.bfloat16)


def places(slots, rows):
    vmem = pl.BlockSpec(memory_space=pltpu.VMEM)
    return pl.pallas_call(
        places_kernel,
        out_shape=jax.ShapeDtypeStruct((rows, slots.shape[1]), jnp.bfloat16),
        in_specs=[vmem],
        out_specs=vmem,
        cost_estimate=pl.CostEstimate(flops=HINT, bytes_accessed=2 * rows * slots.shape[1], transcendentals=0),
        name="places",
    )(slots)


def weighted(vals, root_weight):
    member_mean = jnp.mean(vals, axis=1, keepdims=True)
    return (root_weight * (vals - member_mean)).astype(jnp.bfloat16)


def on_device(predictions, obs_index, data_values, noise_var, perturbations, unknowns):
    shards = lax.axis_size(AXES)
    rows, members = predictions.shape
    capacity = 2 * rows // shards
    me = lax.axis_index(AXES)
    f32, bf16 = jnp.float32, jnp.bfloat16
    ids = jnp.arange(rows, dtype=jnp.int32)
    shard_ids = jnp.arange(shards, dtype=jnp.int32)
    earlier = (ids[:, None] < ids[None, :]).astype(bf16)

    owners, slots = obs_index // rows, obs_index % rows
    by_owner = (shard_ids[:, None] == owners[None, :]).astype(bf16)
    ahead = jnp.dot(by_owner, earlier, preferred_element_type=f32)
    rank = jnp.sum(ahead * by_owner.astype(f32), axis=0).astype(jnp.int32)
    place = owners * capacity + rank
    pack = (jnp.arange(shards * capacity, dtype=jnp.int32)[:, None] == place[None, :]).astype(bf16)
    outgoing = jnp.dot(pack, predictions, preferred_element_type=f32).astype(bf16)
    got = lax.all_to_all(outgoing.reshape(shards, capacity, members), AXES, split_axis=0, concat_axis=0, tiled=True)

    own = jnp.stack([obs_index.astype(f32), noise_var])[None]
    table = lax.all_to_all(jnp.broadcast_to(own, (shards, 2, rows)), AXES, split_axis=0, concat_axis=0, tiled=True)[None]
    table = after(table, outgoing)
    index_table, noise_table = table[0, :, 0].astype(jnp.int32), table[0, :, 1]

    noise_rows = jnp.dot(by_owner.T.astype(f32), noise_table, precision=lax.Precision.HIGHEST, preferred_element_type=f32)
    noise_here = jnp.sum(jnp.where(slots[:, None] == ids[None, :], noise_rows, 0.0), axis=1, keepdims=True)
    here = weighted(predictions.astype(f32), jnp.sqrt(1.0 / noise_here))
    tiles = jnp.concatenate(
        [
            jnp.dot(here[:, j:].T, here[:, j : j + TILE], preferred_element_type=f32)
            for j in range(0, members, TILE)
        ]
    )
    mine = index_table // rows == me
    mine_ahead = jnp.dot(mine.astype(bf16), earlier, preferred_element_type=f32).astype(jnp.int32)
    chosen = mine[:, None, :] & (mine_ahead[:, None, :] == jnp.arange(capacity, dtype=jnp.int32)[None, :, None])
    slot_of = jnp.sum(jnp.where(chosen, index_table[:, None, :] % rows + 1, 0), axis=2).reshape(1, -1) - 1
    unpack = places(slot_of, rows)
    last = stages()[2][-1]
    ahead_steps = steps_of(halve)[:-1] + [lambda parts: (merged(parts) + swap(merged(parts), last),)] + steps_of(double)[-2:0:-1]
    gram = (tiles.reshape(2, -1, TILE),)
    for i, step in enumerate(ahead_steps[:HOLD]):
        gram = step(gram)
        if i == 0:
            gram = after(gram, unpack)

    arranged = jnp.dot(unpack, got.reshape(-1, members), preferred_element_type=f32).astype(bf16)

    pred_vals = arranged.astype(f32)
    root_weight = jnp.sqrt(1.0 / noise_var)[:, None]
    anomalies = weighted(pred_vals, root_weight)
    raw_innov = data_values[:, None] + perturbations.astype(f32) - pred_vals
    innovation_var = jnp.mean(raw_innov * raw_innov, axis=1)
    innovation = (root_weight * raw_innov).astype(bf16)

    head = stages()[0]
    bit = my_bit(head)
    wide = members // 2

    def cross_part(side):
        cols = lax.dynamic_slice_in_dim(innovation, side * wide, wide, 1)
        return jnp.dot(cols.T, anomalies, preferred_element_type=f32).reshape(2, -1, members)


    later = iter(ahead_steps[HOLD:])
    gram, send = lax.optimization_barrier((gram, cross_part(1 - bit)))
    cross = (cross_part(bit) + swap(send, head),)
    gram = next(later)(gram)
    for i, step in enumerate(steps_of(halve)[1:]):
        cross = step(cross)
        if i == 0:
            gram = after(gram, cross[0])
        gram = next(later, lambda parts: parts)(gram)
    for step in later:
        gram = step(gram)
    near, cross = lax.optimization_barrier((merged(gram), merged(cross)))
    side = jnp.reshape(bit, (1,)).astype(jnp.int32)
    gain = solve(side, near, swap(near, head), cross.reshape(-1, members)).reshape(2, -1, members)

    gain = (gather(gain, "obs"),)
    block = after(unknowns, gain)
    block_vals = block.astype(f32)
    spread = (block_vals - jnp.mean(block_vals, axis=1, keepdims=True)).astype(bf16)
    for step in steps_of(double)[len(stages()[1][0]) : 0 : -1]:
        gain = step(gain)
    gain = merged(gain).reshape(wide, members)
    other = swap(gain, head)

    def side_of(gain, at):
        moved = lax.dot_general(spread, gain, (((1,), (1,)), ((), ())), preferred_element_type=f32)
        return (lax.dynamic_slice_in_dim(block, at, wide, 1).astype(f32) + moved).astype(bf16)

    updated = lax.dynamic_update_slice_in_dim(jnp.zeros_like(unknowns), side_of(gain, bit * wide), bit * wide, 1)
    updated = lax.dynamic_update_slice_in_dim(updated, side_of(other, (1 - bit) * wide), (1 - bit) * wide, 1)
    return (updated, innovation_var)


def solution(mesh):
    return jax.shard_map(
        on_device,
        mesh=mesh,
        in_specs=(
            P(AXES, None),
            P(AXES),
            P(AXES),
            P(AXES),
            P(AXES, None),
            P(AXES, None),
        ),
        out_specs=(P(AXES, None), P(AXES)),
        check_vma=False,
    )
```

```python
import functools
import jax
import jax.numpy as jnp
from jax import lax
from jax.experimental import pallas as pl
from jax.experimental.pallas import tpu as pltpu
from jax.sharding import PartitionSpec as P

AXES = ("state", "obs")
TILE = 256
TOLERANCE = 5e-4
STEPS = 512
ROUNDS = 32
FIRST_STEPS = 4
HINT = 20000000000
HOLD = 4


def bits_of(axis):
    return [(axis, b) for b in range(lax.axis_size(axis).bit_length() - 1)]


def my_bit(dim):
    axis, b = dim
    return (lax.axis_index(axis) >> b) & 1


def swap(vals, dim):
    axis, b = dim
    return lax.ppermute(vals, axis, [(i, i ^ (1 << b)) for i in range(lax.axis_size(axis))])


def halves(vals, bit):
    half = vals.shape[1] // 2
    return tuple(lax.dynamic_slice_in_dim(vals, b * half, half, 1) for b in (bit, 1 - bit))


def halve(vals, dim):
    keep, send = halves(vals, my_bit(dim))
    return keep + swap(send, dim)


def halve_sum(one, other, dim):
    bit = my_bit(dim)
    (keep, send), (keep_other, send_other) = halves(one, bit), halves(other, bit)
    return keep + keep_other + swap(send + send_other, dim)


def double(vals, dim):
    other = swap(vals, dim)
    low = my_bit(dim) == 0
    return jnp.concatenate([jnp.where(low, vals, other), jnp.where(low, other, vals)], axis=1)


def gather(vals, axis):
    count, mine = lax.axis_size(axis), lax.axis_index(axis)
    pairs = lambda flip: [(i, i ^ flip) for i in range(count)]
    got = [vals] + [lax.ppermute(vals, axis, pairs(flip)) for flip in range(1, count)]
    bits = count.bit_length() - 1
    in_order = [sum((i >> b & 1) << (bits - 1 - b) for b in range(bits)) for i in range(count)]
    return jnp.concatenate([lax.select_n(mine ^ i, *got) for i in in_order], axis=1)


def stages():
    state, obs = bits_of("state"), bits_of("obs")
    return state[0], (state[1:], state[1:][::-1]), obs


def merged(parts):
    return parts[0] if len(parts) == 1 else jnp.concatenate(parts)


def parted(parts):
    return parts if len(parts) == 2 else (parts[0][:1], parts[0][1:])


def steps_of(exchange):
    head, middle, tail = stages()

    def both(dim):
        return lambda parts: (exchange(merged(parts), dim),)

    def each(dims):
        return lambda parts: tuple(exchange(v, dim) for v, dim in zip(parted(parts), dims, strict=True))

    return [both(head)] + [each(dims) for dims in zip(*middle, strict=True)] + [both(dim) for dim in tail]


def after(vals, first):
    return lax.optimization_barrier((vals, first))[0]


def tile_starts(members):
    starts, at = [], 0
    for j in range(members // TILE):
        starts.append(at)
        at += members - j * TILE
    return starts, at


def solve_kernel(bit_ref, near_ref, far_ref, rhs_ref, out_ref, tiles_ref, s1_ref, s2_ref, s3_ref, diag_ref):
    count, members = rhs_ref.shape
    shift = float(members - 1)
    starts, _ = tile_starts(members)
    blocks = members // TILE
    row = lax.broadcasted_iota(jnp.int32, (TILE, TILE), 0)
    col = lax.broadcasted_iota(jnp.int32, (TILE, TILE), 1)

    def place(vals, i, j):
        here = (pl.ds(i * TILE, TILE), pl.ds(j * TILE, TILE))
        one = vals.astype(jnp.bfloat16)
        rest = vals - one.astype(jnp.float32)
        two = rest.astype(jnp.bfloat16)
        s1_ref[here] = one
        s2_ref[here] = two
        s3_ref[here] = (rest - two.astype(jnp.float32)).astype(jnp.bfloat16)

    streams, half, _ = near_ref.shape
    for s in range(streams):
        for side, ref in ((bit_ref[0], near_ref), (1 - bit_ref[0], far_ref)):
            tiles_ref[pl.ds(pl.multiple_of((2 * s + side) * half, 8), half), :] = ref[s]

    for j in range(blocks):
        for i in range(j, blocks):
            vals = tiles_ref[pl.ds(starts[j] + (i - j) * TILE, TILE), :]
            if i == j:
                on = jnp.where(row == col, vals, 0.0)
                diag_ref[:, pl.ds(j * TILE, TILE)] = jnp.sum(on, axis=0, keepdims=True) + shift
                place(vals - on, j, j)
            else:
                place(vals, i, j)
                place(vals.T, j, i)

    diag = diag_ref[...]
    inverse = 1.0 / diag
    rhs = rhs_ref[...]
    dot = functools.partial(jnp.dot, preferred_element_type=jnp.float32)

    def split(vals):
        one = vals.astype(jnp.bfloat16)
        rest = vals - one.astype(jnp.float32)
        return one, rest.astype(jnp.bfloat16), rest

    def times(vals):
        one, two, rest = split(vals)
        three = (rest - two.astype(jnp.float32)).astype(jnp.bfloat16)
        first = dot(jnp.concatenate([one, two, three]), s1_ref[...])
        second = dot(jnp.concatenate([one, two]), s2_ref[...])
        third = dot(one, s3_ref[...])
        small = first[2 * count :] + second[count:] + third
        return vals * diag + (first[:count] + (first[count : 2 * count] + second[:count] + small))

    def nearly_times(vals):
        one, two, _ = split(vals)
        first = dot(jnp.concatenate([one, two]), s1_ref[...])
        return vals * diag + (first[:count] + first[count:])

    bound = (TOLERANCE * shift) ** 2

    def unsolved(x, r):
        gap = jnp.sum(r * r, axis=1, keepdims=True) - bound * jnp.sum(x * x, axis=1, keepdims=True)
        return jnp.max(gap)

    def divide(a, b):
        return jnp.where(b > 0.0, a / jnp.where(b > 0.0, b, 1.0), 0.0)

    def step_of(product, x, r, p, rz):
        q = product(p)
        alpha = divide(rz, jnp.sum(p * q, axis=1, keepdims=True))
        return x + alpha * p, r - alpha * q

    def turn(r, p, rz):
        z = r * inverse
        rz_next = jnp.sum(r * z, axis=1, keepdims=True)
        return z + divide(rz_next, rz) * p, rz_next

    x, r = jnp.zeros_like(rhs), rhs
    p, rz = turn(r, r, jnp.zeros((count, 1), jnp.float32))
    for i in range(FIRST_STEPS):
        x, r = step_of(nearly_times, x, r, p, rz)
        if i < FIRST_STEPS - 1:
            p, rz = turn(r, p, rz)

    def norm(r):
        return jnp.sum(r * r, axis=1, keepdims=True)

    def keep_better(x, r, new_x):
        new_r = rhs - times(new_x)
        better = norm(new_r) < norm(r)
        progress = jnp.max(jnp.where(norm(new_r) < 0.5 * norm(r), 1, 0))
        return jnp.where(better, new_x, x), jnp.where(better, new_r, r), progress

    r = rhs - times(x)

    def more(carry):
        return jnp.logical_and(carry[0] < STEPS, carry[1] > 0.0)

    def advance(carry):
        step, _, x, r, p, rz = carry
        x, r = step_of(times, x, r, p, rz)
        p, rz = turn(r, p, rz)
        return step + 1, unsolved(x, r), x, r, p, rz

    def more_rounds(carry):
        count, gap, progress = carry[:3]
        return jnp.logical_and(jnp.logical_and(count < ROUNDS, gap > 0.0), progress > 0)

    def another(carry):
        count, gap, _, x, r = carry
        p, rz = turn(r, r, jnp.zeros((rhs.shape[0], 1), jnp.float32))
        new_x = lax.while_loop(more, advance, (jnp.int32(0), gap, x, r, p, rz))[2]
        x, r, progress = keep_better(x, r, new_x)
        return count + 1, unsolved(x, r), progress, x, r

    x = lax.while_loop(more_rounds, another, (jnp.int32(0), unsolved(x, r), jnp.int32(1), x, r))[3]
    out_ref[...] = x.astype(jnp.bfloat16)


def solve(bit, near, far, rhs):
    members = rhs.shape[1]
    square = pltpu.VMEM((members, members), jnp.bfloat16)
    vmem = pl.BlockSpec(memory_space=pltpu.VMEM)
    return pl.pallas_call(
        solve_kernel,
        out_shape=jax.ShapeDtypeStruct(rhs.shape, jnp.bfloat16),
        in_specs=[pl.BlockSpec(memory_space=pltpu.SMEM), vmem, vmem, vmem],
        out_specs=vmem,
        scratch_shapes=[
            pltpu.VMEM((tile_starts(members)[1], TILE), jnp.float32),
            square,
            square,
            square,
            pltpu.VMEM((1, members), jnp.float32),
        ],
        compiler_params=pltpu.CompilerParams(vmem_limit_bytes=20 * 1024 * 1024),
        cost_estimate=pl.CostEstimate(flops=24 * 2 * rhs.shape[0] * members * members, bytes_accessed=6 * members * members, transcendentals=0),
        name="member_solve",
    )(bit, near, far, rhs)


def places_kernel(slot_ref, out_ref):
    ids = lax.broadcasted_iota(jnp.int32, out_ref.shape, 0)
    out_ref[...] = jnp.where(ids == slot_ref[...], 1.0, 0.0).astype(jnp.bfloat16)


def places(slots, rows):
    vmem = pl.BlockSpec(memory_space=pltpu.VMEM)
    return pl.pallas_call(
        places_kernel,
        out_shape=jax.ShapeDtypeStruct((rows, slots.shape[1]), jnp.bfloat16),
        in_specs=[vmem],
        out_specs=vmem,
        cost_estimate=pl.CostEstimate(flops=HINT, bytes_accessed=2 * rows * slots.shape[1], transcendentals=0),
        name="places",
    )(slots)


def weighted(vals, root_weight):
    member_mean = jnp.mean(vals, axis=1, keepdims=True)
    return (root_weight * (vals - member_mean)).astype(jnp.bfloat16)


def on_device(predictions, obs_index, data_values, noise_var, perturbations, unknowns):
    shards = lax.axis_size(AXES)
    rows, members = predictions.shape
    capacity = 2 * rows // shards
    me = lax.axis_index(AXES)
    f32, bf16 = jnp.float32, jnp.bfloat16
    ids = jnp.arange(rows, dtype=jnp.int32)
    shard_ids = jnp.arange(shards, dtype=jnp.int32)
    earlier = (ids[:, None] < ids[None, :]).astype(bf16)

    owners, slots = obs_index // rows, obs_index % rows
    by_owner = (shard_ids[:, None] == owners[None, :]).astype(bf16)
    ahead = jnp.dot(by_owner, earlier, preferred_element_type=f32)
    rank = jnp.sum(ahead * by_owner.astype(f32), axis=0).astype(jnp.int32)
    place = owners * capacity + rank
    pack = (jnp.arange(shards * capacity, dtype=jnp.int32)[:, None] == place[None, :]).astype(bf16)
    outgoing = jnp.dot(pack, predictions, preferred_element_type=f32).astype(bf16)
    got = lax.all_to_all(outgoing.reshape(shards, capacity, members), AXES, split_axis=0, concat_axis=0, tiled=True)

    own = jnp.stack([obs_index.astype(f32), noise_var])[None]
    table = lax.all_to_all(jnp.broadcast_to(own, (shards, 2, rows)), AXES, split_axis=0, concat_axis=0, tiled=True)[None]
    table = after(table, outgoing)
    index_table, noise_table = table[0, :, 0].astype(jnp.int32), table[0, :, 1]

    noise_rows = jnp.dot(by_owner.T.astype(f32), noise_table, precision=lax.Precision.HIGHEST, preferred_element_type=f32)
    noise_here = jnp.sum(jnp.where(slots[:, None] == ids[None, :], noise_rows, 0.0), axis=1, keepdims=True)
    here = weighted(predictions.astype(f32), jnp.sqrt(1.0 / noise_here))
    tiles = jnp.concatenate(
        [
            jnp.dot(here[:, j:].T, here[:, j : j + TILE], preferred_element_type=f32)
            for j in range(0, members, TILE)
        ]
    )
    mine = index_table // rows == me
    mine_ahead = jnp.dot(mine.astype(bf16), earlier, preferred_element_type=f32).astype(jnp.int32)
    chosen = mine[:, None, :] & (mine_ahead[:, None, :] == jnp.arange(capacity, dtype=jnp.int32)[None, :, None])
    slot_of = jnp.sum(jnp.where(chosen, index_table[:, None, :] % rows + 1, 0), axis=2).reshape(1, -1) - 1
    unpack = places(slot_of, rows)
    last = stages()[2][-1]
    ahead_steps = steps_of(halve)[:-1] + [lambda parts: (merged(parts) + swap(merged(parts), last),)] + steps_of(double)[-2:0:-1]
    gram = (tiles.reshape(2, -1, TILE),)
    for i, step in enumerate(ahead_steps[:HOLD]):
        gram = step(gram)
        if i == 0:
            gram = after(gram, unpack)

    arranged = jnp.dot(unpack, got.reshape(-1, members), preferred_element_type=f32).astype(bf16)

    pred_vals = arranged.astype(f32)
    root_weight = jnp.sqrt(1.0 / noise_var)[:, None]
    anomalies = weighted(pred_vals, root_weight)
    raw_innov = data_values[:, None] + perturbations.astype(f32) - pred_vals
    innovation_var = jnp.mean(raw_innov * raw_innov, axis=1)
    innovation = (root_weight * raw_innov).astype(bf16)

    head = stages()[0]
    bit = my_bit(head)
    wide = members // 2

    def cross_part(side):
        cols = lax.dynamic_slice_in_dim(innovation, side * wide, wide, 1)
        return jnp.dot(cols.T, anomalies, preferred_element_type=f32).reshape(2, -1, members)


    later = iter(ahead_steps[HOLD:])
    gram, send = lax.optimization_barrier((gram, cross_part(1 - bit)))
    kept, came = cross_part(bit), swap(send, head)
    cross = None
    gram = next(later)(gram)
    for i, step in enumerate(steps_of(halve)[1:]):
        if i == 0:
            dims = next(zip(*stages()[1], strict=True))
            cross = tuple(halve_sum(kept[n : n + 1], came[n : n + 1], dim) for n, dim in enumerate(dims))
        else:
            cross = step(cross)
        if i == 0:
            gram = after(gram, cross[0])
        gram = next(later, lambda parts: parts)(gram)
    for step in later:
        gram = step(gram)
    near, cross = lax.optimization_barrier((merged(gram), merged(cross)))
    side = jnp.reshape(bit, (1,)).astype(jnp.int32)
    gain = solve(side, near, swap(near, head), cross.reshape(-1, members)).reshape(2, -1, members)

    gain = (gather(gain, "obs"),)
    block = after(unknowns, gain)
    block_vals = block.astype(f32)
    spread = (block_vals - jnp.mean(block_vals, axis=1, keepdims=True)).astype(bf16)
    for step in steps_of(double)[len(stages()[1][0]) : 0 : -1]:
        gain = step(gain)
    gain = merged(gain).reshape(wide, members)
    other = swap(gain, head)

    def side_of(gain, at):
        moved = lax.dot_general(spread, gain, (((1,), (1,)), ((), ())), preferred_element_type=f32)
        return (lax.dynamic_slice_in_dim(block, at, wide, 1).astype(f32) + moved).astype(bf16)

    updated = lax.dynamic_update_slice_in_dim(jnp.zeros_like(unknowns), side_of(gain, bit * wide), bit * wide, 1)
    updated = lax.dynamic_update_slice_in_dim(updated, side_of(other, (1 - bit) * wide), (1 - bit) * wide, 1)
    return (updated, innovation_var)


def solution(mesh):
    return jax.shard_map(
        on_device,
        mesh=mesh,
        in_specs=(
            P(AXES, None),
            P(AXES),
            P(AXES),
            P(AXES),
            P(AXES, None),
            P(AXES, None),
        ),
        out_specs=(P(AXES, None), P(AXES)),
        check_vma=False,
    )
```
